32 devices in a mesh: pages: 8 (over z, x), query: 4 (over y, core).
Axes of the slice: x: 2, y: 2, z: 4, core: 2. Of those that a mesh axis runs over, the one named last changes fastest.
Arguments:
- queries: bfloat16 [8, 48, 32, 128], P('pages', 'query'), may hold values from -8 to 8
- pages: bfloat16 [128, 1024, 128], P('pages', 'query'), may hold values from -8 to 8
- cand_owner: int32 [8, 3], P('pages'), may hold values from 0 to 7, all different within a row
- cand_slot: int32 [8, 3], P('pages'), may hold values from 0 to 15
Outputs:
- losses: float32 [8, 48], P('pages', 'query')
- query_grad: float32 [8, 48, 32, 128], P('pages', 'query')
- page_grad: float32 [128, 1024, 128], P('pages', 'query')
The draws below stay inside these ranges and needn't reach their ends.
Inputs may be any that keep to these rules, and one draw needn't show every extreme that they name: `cand_owner`: each row names 3 different owner indices, and every index is named by some row.
All inputs are finite; a program needn't handle non-finite values.
Results may differ from the reference program's by a relative error of at most 0.0024.
Values may be sent and summed in bfloat16 or wider, within the bound.
A program may use at most 64 MiB of HBM per device.

```python
import jax
import jax.numpy as jnp
from jax import lax

E = 128
PATCHES = 1024
QB = 48
QT = 32
PG_DEV = 16
C = 3
NB = 8
NPAGE = 128
N_PAGES = 8


def shared_direction(key):
    direction = jax.random.normal(jax.random.fold_in(key, 7101), (E,), jnp.float32)
    return direction / jnp.sqrt(jnp.sum(direction * direction))


def draw_queries(key, part):
    direction = shared_direction(key)
    shape = (NB, QB, QT, E)
    noise_key = jax.random.fold_in(key, 211)
    level_key = jax.random.fold_in(key, 223)
    token_key = jax.random.fold_in(key, 227)
    noise = jnp.clip(jax.random.normal(noise_key, shape, jnp.float32), -4.0, 4.0)
    query_level = jax.random.uniform(level_key, (NB, QB, 1, 1), jnp.float32, 0.3, 1.1)
    token_level = jax.random.uniform(token_key, (NB, QB, QT, 1), jnp.float32, 0.5, 1.5)
    values = noise + query_level * token_level * E ** 0.5 * direction
    return jnp.clip(values, -8.0, 8.0).astype(jnp.bfloat16)


def draw_pages(key, part):
    direction = shared_direction(key)
    shape = (NPAGE, PATCHES, E)
    noise_key = jax.random.fold_in(key, 307)
    level_key = jax.random.fold_in(key, 311)
    patch_key = jax.random.fold_in(key, 313)
    noise = jnp.clip(jax.random.normal(noise_key, shape, jnp.float32), -4.0, 4.0)
    page_level = jax.random.uniform(level_key, (NPAGE, 1, 1), jnp.float32, 0.0, 0.9)
    patch_level = jax.random.uniform(patch_key, (NPAGE, PATCHES, 1), jnp.float32, 0.3, 1.7)
    values = noise + page_level * patch_level * E ** 0.5 * direction
    return jnp.clip(values, -8.0, 8.0).astype(jnp.bfloat16)


def touch_ends(values, key, least, top_value):
    index_at = [jax.random.randint(jax.random.fold_in(key, axis), (), 0, length) for axis, length in enumerate(values.shape)]
    main_axis = values.shape.index(max(values.shape))
    next_to = index_at[:main_axis] + [(index_at[main_axis] + 1) % values.shape[main_axis]] + index_at[main_axis + 1:]
    return values.at[tuple(index_at)].set(least).at[tuple(next_to)].set(top_value)


def choose_distinct(own_key, rows, number_of, top, lift):
    order = jax.random.permutation(jax.random.fold_in(own_key, 1), number_of)
    boost = order
    for power in range(3):
        boost = boost * boost // number_of
    boost = boost * lift // number_of
    lots = jax.random.randint(jax.random.fold_in(own_key, 2), (rows, number_of), 0, 4096) + boost
    sure = jax.random.permutation(jax.random.fold_in(own_key, 3), rows)[jnp.arange(number_of) % rows]
    lots = jnp.where(jnp.arange(rows)[:, None] == sure[None, :], 1 << 14, lots)
    merit = lots * number_of + jnp.arange(number_of)
    return lax.top_k(merit.astype(jnp.int32), top)[1].astype(jnp.int32)


def setup_inputs(seed: int = 0) -> dict:
    seeds = jax.random.split(jax.random.key(seed), 5)
    queries = draw_queries(jax.random.fold_in(seeds[4], 71), 0)
    pages = draw_pages(jax.random.fold_in(seeds[4], 71), 0)
    cand_owner = choose_distinct(seeds[2], NB, N_PAGES, C, 6144)
    cand_slot = touch_ends(jax.random.randint(seeds[3], (NB, C), 0, PG_DEV), jax.random.fold_in(seeds[3], 1), 0, PG_DEV - 1).astype(jnp.int32)
    return {"queries": queries, "pages": pages, "cand_owner": cand_owner, "cand_slot": cand_slot}


SHARPNESS = 10.0
INV_TEMP = 20.0
LOSS_SCALE = 256.0
EPSILON = 1e-06

def normalize(embeddings):
    values = embeddings.astype(jnp.float32)
    inverse = lax.rsqrt(lax.optimization_barrier(jnp.sum(values * values, axis=-1, keepdims=True)) + EPSILON)
    return (values * inverse, inverse)

def unnormalize_grad(unit_vectors, inverse, gradient):
    return inverse * (gradient - unit_vectors * lax.optimization_barrier(jnp.sum(unit_vectors * gradient, axis=-1, keepdims=True)))

def coefficients(totals, tokens):
    candidates = totals.shape[0]
    queries_here = totals.shape[1] // tokens
    shaped = totals.reshape(candidates, queries_here, tokens)
    per_token = jnp.log(shaped) / SHARPNESS
    logits = INV_TEMP * lax.optimization_barrier(jnp.mean(per_token, axis=2))
    exponentials = jnp.exp(logits)
    denominator = lax.optimization_barrier(jnp.sum(exponentials, axis=0))
    losses = jnp.log(denominator) - logits[0]
    positive = (jnp.arange(candidates) == 0).astype(jnp.float32)[:, None]
    probability = exponentials / denominator
    scaled = LOSS_SCALE * INV_TEMP / tokens * (probability - positive)
    weights = scaled[:, :, None] / shaped
    return (weights.reshape(candidates, queries_here * tokens), losses)

def reference(queries, pages, cand_owner, cand_slot):
    q_unit, q_inv = normalize(queries)
    d_unit, d_inv = normalize(pages)
    q_round = q_unit.astype(jnp.bfloat16)
    d_round = d_unit.astype(jnp.bfloat16)
    page_id = (cand_owner * PG_DEV + cand_slot).astype(jnp.int32)

    def one_block(page_back, element):
        block_tokens, identities = element
        query_rows = block_tokens.reshape(QB * QT, E)
        chosen = jnp.take(d_round, identities, axis=0)

        def forward(unused, page_piece):
            scores = jnp.dot(query_rows, page_piece.T, preferred_element_type=jnp.float32)
            return (unused, lax.optimization_barrier(jnp.sum(jnp.exp(SHARPNESS * scores), axis=1)))
        _, totals = lax.scan(forward, None, chosen)
        weights, losses = coefficients(totals, QT)

        def backward(grad_rows, pair):
            page_piece, weight_row = pair
            scores = jnp.dot(query_rows, page_piece.T, preferred_element_type=jnp.float32)
            shares = (weight_row[:, None] * jnp.exp(SHARPNESS * scores)).astype(jnp.bfloat16)
            grad_rows = grad_rows + jnp.dot(shares, page_piece, preferred_element_type=jnp.float32)
            page_term = jnp.dot(shares.T, query_rows, preferred_element_type=jnp.float32)
            return (grad_rows, page_term)
        grad_rows, page_terms = lax.scan(backward, jnp.zeros((QB * QT, E), jnp.float32), (chosen, weights))
        page_back = page_back.at[identities].add(page_terms)
        return (page_back, (grad_rows.reshape(QB, QT, E), losses))
    start = jnp.zeros(pages.shape, jnp.float32)
    page_back, (query_back, losses) = lax.scan(one_block, start, (q_round, page_id))
    query_grad = unnormalize_grad(q_unit, q_inv, query_back)
    page_grad = unnormalize_grad(d_unit, d_inv, page_back)
    return (losses, query_grad, page_grad)
```

```python
import functools
import math

import jax
import jax.numpy as jnp
from jax import lax
from jax.experimental import pallas as pl
from jax.experimental.pallas import tpu as pltpu
from jax.sharding import PartitionSpec as P

SHARPNESS = 10.0
INV_TEMP = 20.0
LOSS_SCALE = 256.0
EPSILON = 1e-06
LANES = 128
MESH = pl.DeviceIdType.MESH
VMEM_BYTES = 56 * 2**20
F32 = jnp.float32
BF16 = jnp.bfloat16


def normalize(embeddings):
    values = embeddings.astype(F32)
    inverse = lax.rsqrt(jnp.sum(values * values, axis=-1, keepdims=True) + EPSILON)
    return values * inverse, inverse


def unnormalize_grad(unit_vectors, inverse, gradient):
    return inverse * (
        gradient - unit_vectors * jnp.sum(unit_vectors * gradient, axis=-1, keepdims=True)
    )


def group_sums(values, size):
    width = values.shape[1]
    lane = lax.broadcasted_iota(jnp.int32, values.shape, 1)
    step = 1
    while step < size:
        upper = (lane & step) != 0
        values = values + jnp.where(
            upper, pltpu.roll(values, step, 1), pltpu.roll(values, width - step, 1)
        )
        step *= 2
    return values


def exchange_kernel(
    owners, groups, candidates, tokens,
    q_ref, pages_ref, owner_ref, slot_ref,
    loss_ref, qgrad_ref, back_ref, asked_ref,
    q_all, d_round, asked, asked_smem, send, fetched, turned, sums, rows_ref, weight_ref,
    shares, terms, q_part, q_got,
    ask_out, ask_in, page_out, page_in, back_out, back_in,
    q_out, q_in, sum_out, sum_in, part_out, part_in, local_sem,
):
    me = lax.axis_index("pages")
    mine = lax.axis_index("query")
    page_count = pages_ref.shape[0]
    rows = q_ref.shape[0]
    padded = rows_ref.shape[0]

    def to_owner(k):
        return lax.rem(me + k, owners)

    def from_owner(k):
        return lax.rem(me + owners - k, owners)

    def to_group(k):
        return lax.rem(mine + k, groups)

    def from_group(k):
        return lax.rem(mine + groups - k, groups)

    def across_pages(src, dst, out, into, k):
        return pltpu.make_async_remote_copy(
            src_ref=src, dst_ref=dst, send_sem=out.at[k], recv_sem=into.at[k],
            device_id=(to_owner(k), mine), device_id_type=MESH,
        )

    def across_query(src, dst, out, into, k):
        return pltpu.make_async_remote_copy(
            src_ref=src, dst_ref=dst, send_sem=out.at[k], recv_sem=into.at[k],
            device_id=(me, to_group(k)), device_id_type=MESH,
        )

    def each(count, body):
        lax.fori_loop(1, count, lambda k, c: (body(k), c)[1], 0)

    barrier = pltpu.get_barrier_semaphore()
    each(owners, lambda k: pl.semaphore_signal(
        barrier, inc=1, device_id=(to_owner(k), mine), device_id_type=MESH))
    each(groups, lambda k: pl.semaphore_signal(
        barrier, inc=1, device_id=(me, to_group(k)), device_id_type=MESH))

    lane = lax.broadcasted_iota(jnp.int32, (1, LANES), 1)
    wanted = jnp.full((1, LANES), -1, jnp.int32)
    for c in range(candidates):
        wanted = jnp.where(lane == owner_ref[0, c], slot_ref[0, c], wanted)
    asked[me] = wanted
    q_unit, q_inv = normalize(q_ref[...])
    q_all[mine] = q_unit.astype(BF16)
    pl.semaphore_wait(barrier, owners + groups - 2)

    each(owners, lambda k: across_pages(asked.at[me], asked.at[me], ask_out, ask_in, k).start())
    each(groups, lambda k: across_query(q_all.at[mine], q_all.at[mine], q_out, q_in, k).start())

    def round_page(j, carry):
        d_round[j] = normalize(pages_ref[j])[0].astype(BF16)
        return carry

    lax.fori_loop(0, page_count, round_page, 0)

    def ask_arrived(k):
        across_pages(asked.at[from_owner(k)], asked.at[from_owner(k)], ask_out, ask_in, k).wait_recv()
        across_pages(asked.at[me], asked.at[me], ask_out, ask_in, k).wait_send()

    each(owners, ask_arrived)
    to_scalars = pltpu.make_async_copy(asked, asked_smem, local_sem)
    to_scalars.start()
    asked_ref[...] = asked[...]
    to_scalars.wait()

    def serve(k):
        to = to_owner(k)
        send[k] = d_round[jnp.maximum(asked_smem[to, 0, me], 0)]
        across_pages(send.at[k], fetched.at[me], page_out, page_in, k).start()

    each(owners, serve)
    fetched[me] = d_round[jnp.maximum(asked_smem[me, 0, me], 0)]

    def query_arrived(k):
        across_query(q_all.at[from_group(k)], q_all.at[from_group(k)], q_out, q_in, k).wait_recv()
        across_query(q_all.at[mine], q_all.at[mine], q_out, q_in, k).wait_send()

    each(groups, query_arrived)

    def page_arrived(k):
        across_pages(send.at[k], fetched.at[from_owner(k)], page_out, page_in, k).wait()

    each(owners, page_arrived)

    def exponentials(page, g):
        scores = lax.dot_general(
            page, q_all[g], (((1,), (1,)), ((), ())), preferred_element_type=F32
        )
        return jnp.exp2(scores * (SHARPNESS * math.log2(math.e)))

    def forward(c, carry):
        page = fetched[owner_ref[0, c]]
        turned[c] = page.T
        for g in range(groups):
            sums[mine, c, :, g * rows : (g + 1) * rows] = jnp.sum(
                exponentials(page, g), axis=0, keepdims=True
            )
        return carry

    lax.fori_loop(0, candidates, forward, 0)
    each(groups, lambda k: across_query(sums.at[mine], sums.at[mine], sum_out, sum_in, k).start())

    def sums_arrived(k):
        across_query(sums.at[from_group(k)], sums.at[from_group(k)], sum_out, sum_in, k).wait_recv()
        across_query(sums.at[mine], sums.at[mine], sum_out, sum_in, k).wait_send()

    each(groups, sums_arrived)

    rows_ref[...] = jnp.ones_like(rows_ref)
    for c in range(candidates):
        total = sums[0, c]
        for g in range(1, groups):
            total = total + sums[g, c]
        rows_ref[c : c + 1, :] = total
    totals = rows_ref[...]
    logits = (INV_TEMP / SHARPNESS / tokens) * group_sums(jnp.log(totals), tokens)
    which = lax.broadcasted_iota(jnp.int32, totals.shape, 0)
    powers = jnp.where(which < candidates, jnp.exp(logits), 0.0)
    denominator = jnp.sum(powers, axis=0, keepdims=True)
    losses = jnp.log(denominator) - logits[0:1]
    positive = jnp.where(which == 0, 1.0, 0.0)
    weights = (LOSS_SCALE * INV_TEMP / tokens) * (powers / denominator - positive) / totals
    for g in range(groups):
        loss_ref[g] = losses[:, g * rows : (g + 1) * rows]
    for c in range(candidates):
        weight_ref[c] = weights[c : c + 1]

    def backward(c, carry):
        page = fetched[owner_ref[0, c]]
        term = jnp.zeros(page.shape, F32)
        for g in range(groups):
            share = (
                weight_ref[c, :, g * rows : (g + 1) * rows] * exponentials(page, g)
            ).astype(BF16)
            shares[c, g] = share
            term = term + jnp.dot(share, q_all[g], preferred_element_type=F32)
        terms[c] = term.astype(BF16)
        return carry

    lax.fori_loop(0, candidates, backward, 0)

    def term_for(owner):
        place = jnp.int32(0)
        for c in range(candidates):
            place = jnp.where(owner_ref[0, c] == owner, c, place)
        return terms[place]

    def give_back(k):
        send[k] = term_for(to_owner(k))
        across_pages(send.at[k], back_ref.at[me], back_out, back_in, k).start()

    each(owners, give_back)
    back_ref[me] = term_for(me)

    for k in range(1, groups + 1):
        g = to_group(k)

        def query_side(c, total, g=g):
            return total + jnp.dot(turned[c], shares[c, g], preferred_element_type=F32)

        q_part[k - 1] = lax.fori_loop(
            0, candidates, query_side, jnp.zeros(q_part.shape[1:], F32)
        )
        if k < groups:
            across_query(q_part.at[k - 1], q_got.at[k - 1], part_out, part_in, k).start()

    total = q_part[groups - 1]
    for k in range(1, groups):
        across_query(q_part.at[k - 1], q_got.at[k - 1], part_out, part_in, k).wait()
        total = total + q_got[k - 1]
    q_unit, q_inv = normalize(q_ref[...])
    qgrad_ref[...] = unnormalize_grad(q_unit, q_inv, total.T)

    def back_arrived(k):
        across_pages(send.at[k], back_ref.at[from_owner(k)], back_out, back_in, k).wait()

    each(owners, back_arrived)


def page_kernel(owners, asked_ref, pages_ref, back_ref, out_ref, total):
    me = lax.axis_index("pages")
    here = pages_ref.shape[0]
    for i in range(here):
        page = pl.program_id(0) * here + i

        def count(r, found):
            return found + jnp.where(asked_ref[r, me] == page, 1, 0)

        found = lax.fori_loop(0, owners, count, jnp.int32(0))

        @pl.when(found == 0)
        def _():
            out_ref[i] = jnp.zeros(out_ref.shape[1:], F32)

        @pl.when(found > 0)
        def _():
            total[...] = jnp.zeros_like(total)

            def add(r, carry):
                @pl.when(asked_ref[r, me] == page)
                def _():
                    total[...] += back_ref[r].astype(F32)

                return carry

            lax.fori_loop(0, owners, add, 0)
            d_unit, d_inv = normalize(pages_ref[i])
            out_ref[i] = unnormalize_grad(d_unit, d_inv, total[...])


def local(queries, pages, cand_owner, cand_slot):
    _, queries_local, tokens, width = queries.shape
    page_count, patches, _ = pages.shape
    owners = lax.axis_size("pages")
    groups = lax.axis_size("query")
    candidates = cand_owner.shape[1]
    rows = queries_local * tokens
    everyone = groups * rows
    padded = -(-candidates // 8) * 8
    dma = pltpu.SemaphoreType.DMA
    vmem = pl.BlockSpec(memory_space=pltpu.VMEM)
    smem = pl.BlockSpec(memory_space=pltpu.SMEM)
    losses, query_grad, back, asked = pl.pallas_call(
        functools.partial(exchange_kernel, owners, groups, candidates, tokens),
        out_shape=(
            jax.ShapeDtypeStruct((groups, 1, rows), F32),
            jax.ShapeDtypeStruct((rows, width), F32),
            jax.ShapeDtypeStruct((owners, patches, width), BF16),
            jax.ShapeDtypeStruct((owners, 1, LANES), jnp.int32),
        ),
        in_specs=[vmem, vmem, smem, smem],
        out_specs=(vmem, vmem, vmem, vmem),
        scratch_shapes=[
            pltpu.VMEM((groups, rows, width), BF16),
            pltpu.VMEM((page_count, patches, width), BF16),
            pltpu.VMEM((owners, 1, LANES), jnp.int32),
            pltpu.SMEM((owners, 1, LANES), jnp.int32),
            pltpu.VMEM((owners, patches, width), BF16),
            pltpu.VMEM((owners, patches, width), BF16),
            pltpu.VMEM((candidates, width, patches), BF16),
            pltpu.VMEM((groups, candidates, 1, everyone), F32),
            pltpu.VMEM((padded, everyone), F32),
            pltpu.VMEM((candidates, 1, everyone), F32),
            pltpu.VMEM((candidates, groups, patches, rows), BF16),
            pltpu.VMEM((candidates, patches, width), BF16),
            pltpu.VMEM((groups, width, rows), F32),
            pltpu.VMEM((groups, width, rows), F32),
        ]
        + [dma((owners,))] * 6
        + [dma((groups,))] * 6
        + [dma],
        compiler_params=pltpu.CompilerParams(
            collective_id=0, has_side_effects=True, vmem_limit_bytes=VMEM_BYTES
        ),
    )(queries.reshape(rows, width), pages, cand_owner, cand_slot)

    block = max(1, page_count // 4)
    whole = pl.BlockSpec((owners, patches, width), lambda i, asked: (0, 0, 0))
    some = pl.BlockSpec((block, patches, width), lambda i, asked: (i, 0, 0))
    page_grad = pl.pallas_call(
        functools.partial(page_kernel, owners),
        out_shape=jax.ShapeDtypeStruct((page_count, patches, width), F32),
        grid_spec=pltpu.PrefetchScalarGridSpec(
            num_scalar_prefetch=1,
            grid=(page_count // block,),
            in_specs=[some, whole],
            out_specs=some,
            scratch_shapes=[pltpu.VMEM((patches, width), F32)],
        ),
        compiler_params=pltpu.CompilerParams(vmem_limit_bytes=VMEM_BYTES),
    )(asked.reshape(owners, LANES), pages, back)
    own = lax.dynamic_index_in_dim(losses, lax.axis_index("query"), 0, keepdims=False)
    return (
        own.reshape(queries_local, tokens)[:, 0][None],
        query_grad.reshape(1, queries_local, tokens, width),
        page_grad,
    )


def solution(mesh):
    return jax.shard_map(
        local,
        mesh=mesh,
        in_specs=(
            P("pages", "query", None, None),
            P("pages", "query", None),
            P("pages", None),
            P("pages", None),
        ),
        out_specs=(P("pages", "query"), P("pages", "query", None, None), P("pages", "query", None)),
        check_vma=False,
    )
```

```python
import functools
import math

import jax
import jax.numpy as jnp
from jax import lax
from jax.experimental import pallas as pl
from jax.experimental.pallas import tpu as pltpu
from jax.sharding import PartitionSpec as P

SHARPNESS = 10.0
INV_TEMP = 20.0
LOSS_SCALE = 256.0
EPSILON = 1e-06
LANES = 128
MESH = pl.DeviceIdType.MESH
VMEM_BYTES = 56 * 2**20
KEEP_BYTES = 8 * 2**20
TILE = 16
F32 = jnp.float32
BF16 = jnp.bfloat16


def normalize(embeddings):
    values = embeddings.astype(F32)
    inverse = lax.rsqrt(jnp.sum(values * values, axis=-1, keepdims=True) + EPSILON)
    return values * inverse, inverse


def unnormalize_grad(unit_vectors, inverse, gradient):
    return inverse * (
        gradient - unit_vectors * jnp.sum(unit_vectors * gradient, axis=-1, keepdims=True)
    )


def group_sums(values, size):
    width = values.shape[1]
    lane = lax.broadcasted_iota(jnp.int32, values.shape, 1)
    step = 1
    while step < size:
        upper = (lane & step) != 0
        values = values + jnp.where(
            upper, pltpu.roll(values, step, 1), pltpu.roll(values, width - step, 1)
        )
        step *= 2
    return values


def exchange_kernel(
    owners, groups, candidates, tokens, keep,
    q_ref, pages_ref, owner_ref, slot_ref,
    loss_ref, qgrad_ref, back_ref, asked_ref,
    q_all, d_round, asked, asked_smem, send, fetched, turned, sums, rows_ref, weight_ref,
    shares, terms, q_part, q_got, kept,
    ask_out, ask_in, page_out, page_in, back_out, back_in,
    q_out, q_in, sum_out, sum_in, part_out, part_in, local_sem,
):
    kept = kept if keep else None
    me = lax.axis_index("pages")
    mine = lax.axis_index("query")
    page_count, patches, width = pages_ref.shape
    rows = q_ref.shape[0]

    def to_owner(k):
        return lax.rem(me + k, owners)

    def from_owner(k):
        return lax.rem(me + owners - k, owners)

    def to_group(k):
        return lax.rem(mine + k, groups)

    def from_group(k):
        return lax.rem(mine + groups - k, groups)

    def across_pages(src, dst, out, into, k):
        return pltpu.make_async_remote_copy(
            src_ref=src, dst_ref=dst, send_sem=out.at[k], recv_sem=into.at[k],
            device_id=(to_owner(k), mine), device_id_type=MESH,
        )

    def across_query(src, dst, out, into, k):
        return pltpu.make_async_remote_copy(
            src_ref=src, dst_ref=dst, send_sem=out.at[k], recv_sem=into.at[k],
            device_id=(me, to_group(k)), device_id_type=MESH,
        )

    def each(count, body):
        lax.fori_loop(1, count, lambda k, c: (body(k), c)[1], 0)

    def far_first(count, body):
        def step(i, carry):
            half = lax.div(i + 1, 2)
            body(jnp.where(lax.rem(i, 2) == 1, count // 2 + half, count // 2 - half))
            return carry

        lax.fori_loop(0, count - 1, step, 0)

    barrier = pltpu.get_barrier_semaphore()
    each(owners, lambda k: pl.semaphore_signal(
        barrier, inc=1, device_id=(to_owner(k), mine), device_id_type=MESH))
    each(groups, lambda k: pl.semaphore_signal(
        barrier, inc=1, device_id=(me, to_group(k)), device_id_type=MESH))

    lane = lax.broadcasted_iota(jnp.int32, (1, LANES), 1)
    wanted = jnp.full((1, LANES), -1, jnp.int32)
    for c in range(candidates):
        wanted = jnp.where(lane == owner_ref[0, c], slot_ref[0, c], wanted)
    asked[me] = wanted
    q_unit, q_inv = normalize(q_ref[...])
    q_all[mine] = q_unit.astype(BF16)
    pl.semaphore_wait(barrier, owners + groups - 2)

    each(owners, lambda k: across_pages(asked.at[me], asked.at[me], ask_out, ask_in, k).start())
    each(groups, lambda k: across_query(q_all.at[mine], q_all.at[mine], q_out, q_in, k).start())

    def round_page(j, carry):
        d_round[j] = normalize(pages_ref[j])[0].astype(BF16)
        return carry

    lax.fori_loop(0, page_count, round_page, 0)

    def ask_arrived(k):
        across_pages(asked.at[from_owner(k)], asked.at[from_owner(k)], ask_out, ask_in, k).wait_recv()
        across_pages(asked.at[me], asked.at[me], ask_out, ask_in, k).wait_send()

    each(owners, ask_arrived)
    to_scalars = pltpu.make_async_copy(asked, asked_smem, local_sem)
    to_scalars.start()
    asked_ref[...] = asked[...]
    to_scalars.wait()

    def serve(k):
        to = to_owner(k)
        send[k, :patches] = d_round[jnp.maximum(asked_smem[to, 0, me], 0)]
        across_pages(
            send.at[k, pl.ds(0, patches)], fetched.at[me], page_out, page_in, k
        ).start()

    far_first(owners, serve)
    fetched[me] = d_round[jnp.maximum(asked_smem[me, 0, me], 0)]

    def query_arrived(k):
        across_query(q_all.at[from_group(k)], q_all.at[from_group(k)], q_out, q_in, k).wait_recv()
        across_query(q_all.at[mine], q_all.at[mine], q_out, q_in, k).wait_send()

    each(groups, query_arrived)

    def page_arrived(k):
        across_pages(
            send.at[k, pl.ds(0, patches)], fetched.at[from_owner(k)], page_out, page_in, k
        ).wait()

    each(owners, page_arrived)

    def exponentials(page, g):
        scores = lax.dot_general(
            page, q_all[g], (((1,), (1,)), ((), ())), preferred_element_type=F32
        )
        return jnp.exp2(scores * (SHARPNESS * math.log2(math.e)))

    def forward(c, carry):
        page = fetched[owner_ref[0, c]]
        turned[c] = page.T
        for g in range(groups):
            powers = exponentials(page, g)
            if kept is not None:
                kept[c, g] = powers
            sums[mine, c, :, g * rows : (g + 1) * rows] = jnp.sum(powers, axis=0, keepdims=True)
        return carry

    lax.fori_loop(0, candidates, forward, 0)
    each(groups, lambda k: across_query(sums.at[mine], sums.at[mine], sum_out, sum_in, k).start())

    def sums_arrived(k):
        across_query(sums.at[from_group(k)], sums.at[from_group(k)], sum_out, sum_in, k).wait_recv()
        across_query(sums.at[mine], sums.at[mine], sum_out, sum_in, k).wait_send()

    each(groups, sums_arrived)

    rows_ref[...] = jnp.ones_like(rows_ref)
    for c in range(candidates):
        total = sums[0, c]
        for g in range(1, groups):
            total = total + sums[g, c]
        rows_ref[c : c + 1, :] = total
    totals = rows_ref[...]
    logits = (INV_TEMP / SHARPNESS / tokens) * group_sums(jnp.log(totals), tokens)
    which = lax.broadcasted_iota(jnp.int32, totals.shape, 0)
    powers = jnp.where(which < candidates, jnp.exp(logits), 0.0)
    denominator = jnp.sum(powers, axis=0, keepdims=True)
    losses = jnp.log(denominator) - logits[0:1]
    positive = jnp.where(which == 0, 1.0, 0.0)
    weights = (LOSS_SCALE * INV_TEMP / tokens) * (powers / denominator - positive) / totals
    own = losses[:, :rows]
    for g in range(1, groups):
        own = jnp.where(mine == g, losses[:, g * rows : (g + 1) * rows], own)
    place = lax.broadcasted_iota(jnp.int32, (LANES, rows), 0)
    token = lax.broadcasted_iota(jnp.int32, (LANES, rows), 1)
    picked = jnp.sum(jnp.where(token == place * tokens, own, 0.0), axis=1, keepdims=True)
    loss_ref[...] = jnp.broadcast_to(picked, (LANES, LANES)).T[:1, : rows // tokens]
    for c in range(candidates):
        weight_ref[c] = weights[c : c + 1]

    def backward(c, carry):
        page = fetched[owner_ref[0, c]]
        term = jnp.zeros(page.shape, F32)
        for g in range(groups):
            powers = exponentials(page, g) if kept is None else kept[c, g]
            share = (weight_ref[c, :, g * rows : (g + 1) * rows] * powers).astype(BF16)
            shares[c, g] = share
            term = term + jnp.dot(share, q_all[g], preferred_element_type=F32)
        values = page.astype(F32)
        along = jnp.sum(values * term, axis=-1, keepdims=True).astype(BF16).astype(F32)
        terms[c, :patches] = (term - values * along).astype(BF16)
        flat = jnp.broadcast_to(along, term.shape).T
        pieces = [flat[:1, i : i + width] for i in range(0, patches, width)]
        pieces.append(jnp.zeros((TILE - len(pieces), width), F32))
        terms[c, patches:] = jnp.concatenate(pieces, axis=0).astype(BF16)
        return carry

    lax.fori_loop(0, candidates, backward, 0)

    def term_for(owner):
        place = jnp.int32(0)
        for c in range(candidates):
            place = jnp.where(owner_ref[0, c] == owner, c, place)
        return terms[place]

    def give_back(k):
        send[k] = term_for(to_owner(k))
        across_pages(send.at[k], back_ref.at[me], back_out, back_in, k).start()

    far_first(owners, give_back)
    back_ref[me] = term_for(me)

    for k in range(1, groups + 1):
        g = to_group(k)

        def query_side(c, total, g=g):
            return total + jnp.dot(turned[c], shares[c, g], preferred_element_type=F32)

        q_part[k - 1] = lax.fori_loop(
            0, candidates, query_side, jnp.zeros(q_part.shape[1:], F32)
        )
        if k < groups:
            across_query(q_part.at[k - 1], q_got.at[k - 1], part_out, part_in, k).start()

    total = q_part[groups - 1]
    for k in range(1, groups):
        across_query(q_part.at[k - 1], q_got.at[k - 1], part_out, part_in, k).wait()
        total = total + q_got[k - 1]
    q_unit, q_inv = normalize(q_ref[...])
    qgrad_ref[...] = unnormalize_grad(q_unit, q_inv, total.T)

    def back_arrived(k):
        across_pages(send.at[k], back_ref.at[from_owner(k)], back_out, back_in, k).wait()

    each(owners, back_arrived)


def finish_kernel(
    owners, asked_ref, pages_ref, back_ref, q_in_ref, loss_in_ref, loss_ref, q_out_ref, out_ref
):
    me = lax.axis_index("pages")
    page_count, patches, width = pages_ref.shape
    loss_ref[...] = loss_in_ref[...]
    q_out_ref[...] = q_in_ref[...]

    def clear(j, carry):
        out_ref[j] = jnp.zeros((patches, width), F32)
        return carry

    lax.fori_loop(0, page_count, clear, 0)

    def add(r, carry):
        slot = asked_ref[r, 0, me]

        @pl.when(slot >= 0)
        def _():
            d_unit, d_inv = normalize(pages_ref[slot])
            flat = back_ref[r, patches:].astype(F32)
            along = jnp.concatenate(
                [
                    jnp.broadcast_to(flat[i : i + 1], (width, width)).T
                    for i in range(patches // width)
                ],
                axis=0,
            )
            term = back_ref[r, :patches].astype(F32) + along * d_unit.astype(BF16).astype(F32)
            out_ref[slot] += unnormalize_grad(d_unit, d_inv, term)

        return carry

    lax.fori_loop(0, owners, add, 0)


def local(queries, pages, cand_owner, cand_slot):
    _, queries_local, tokens, width = queries.shape
    page_count, patches, _ = pages.shape
    owners = lax.axis_size("pages")
    groups = lax.axis_size("query")
    candidates = cand_owner.shape[1]
    rows = queries_local * tokens
    everyone = groups * rows
    padded = -(-candidates // 8) * 8
    assert queries_local <= LANES and owners <= LANES
    assert patches % width == 0 and patches // width < TILE and tokens & (tokens - 1) == 0
    grid = (candidates, groups, patches, rows)
    keep = 4 * math.prod(grid) <= KEEP_BYTES
    dma = pltpu.SemaphoreType.DMA
    vmem = pl.BlockSpec(memory_space=pltpu.VMEM)
    smem = pl.BlockSpec(memory_space=pltpu.SMEM)
    losses, query_grad, back, asked = pl.pallas_call(
        functools.partial(exchange_kernel, owners, groups, candidates, tokens, keep),
        out_shape=(
            jax.ShapeDtypeStruct((1, queries_local), F32),
            jax.ShapeDtypeStruct((rows, width), F32),
            jax.ShapeDtypeStruct((owners, patches + TILE, width), BF16),
            jax.ShapeDtypeStruct((owners, 1, LANES), jnp.int32),
        ),
        in_specs=[vmem, vmem, smem, smem],
        out_specs=(vmem, vmem, vmem, vmem),
        scratch_shapes=[
            pltpu.VMEM((groups, rows, width), BF16),
            pltpu.VMEM((page_count, patches, width), BF16),
            pltpu.VMEM((owners, 1, LANES), jnp.int32),
            pltpu.SMEM((owners, 1, LANES), jnp.int32),
            pltpu.VMEM((owners, patches + TILE, width), BF16),
            pltpu.VMEM((owners, patches, width), BF16),
            pltpu.VMEM((candidates, width, patches), BF16),
            pltpu.VMEM((groups, candidates, 1, everyone), F32),
            pltpu.VMEM((padded, everyone), F32),
            pltpu.VMEM((candidates, 1, everyone), F32),
            pltpu.VMEM(grid, BF16),
            pltpu.VMEM((candidates, patches + TILE, width), BF16),
            pltpu.VMEM((groups, width, rows), F32),
            pltpu.VMEM((groups, width, rows), F32),
            pltpu.VMEM(grid if keep else (8, LANES), F32),
        ]
        + [dma((owners,))] * 6
        + [dma((groups,))] * 6
        + [dma],
        compiler_params=pltpu.CompilerParams(
            collective_id=0, has_side_effects=True, vmem_limit_bytes=VMEM_BYTES
        ),
    )(queries.reshape(rows, width), pages, cand_owner, cand_slot)

    losses, query_grad, page_grad = pl.pallas_call(
        functools.partial(finish_kernel, owners),
        out_shape=(
            jax.ShapeDtypeStruct(losses.shape, F32),
            jax.ShapeDtypeStruct(query_grad.shape, F32),
            jax.ShapeDtypeStruct((page_count, patches, width), F32),
        ),
        in_specs=[smem, vmem, vmem, vmem, vmem],
        out_specs=(vmem, vmem, vmem),
        compiler_params=pltpu.CompilerParams(vmem_limit_bytes=VMEM_BYTES),
    )(asked, pages, back, query_grad, losses)
    return (
        losses,
        query_grad.reshape(1, queries_local, tokens, width),
        page_grad,
    )


def solution(mesh):
    return jax.shard_map(
        local,
        mesh=mesh,
        in_specs=(
            P("pages", "query", None, None),
            P("pages", "query", None),
            P("pages", None),
            P("pages", None),
        ),
        out_specs=(P("pages", "query"), P("pages", "query", None, None), P("pages", "query", None)),
        check_vma=False,
    )
```

```python
import functools
import math

import jax
import jax.numpy as jnp
from jax import lax
from jax.experimental import pallas as pl
from jax.experimental.pallas import tpu as pltpu
from jax.sharding import PartitionSpec as P

SHARPNESS = 10.0
INV_TEMP = 20.0
LOSS_SCALE = 256.0
EPSILON = 1e-06
LANES = 128
MESH = pl.DeviceIdType.MESH
VMEM_BYTES = 56 * 2**20
KEEP_BYTES = 8 * 2**20
TILE = 16
F32 = jnp.float32
BF16 = jnp.bfloat16


def normalize(embeddings):
    values = embeddings.astype(F32)
    inverse = lax.rsqrt(jnp.sum(values * values, axis=-1, keepdims=True) + EPSILON)
    return values * inverse, inverse


def unnormalize_grad(unit_vectors, inverse, gradient):
    return inverse * (
        gradient - unit_vectors * jnp.sum(unit_vectors * gradient, axis=-1, keepdims=True)
    )


def group_sums(values, size):
    width = values.shape[1]
    lane = lax.broadcasted_iota(jnp.int32, values.shape, 1)
    step = 1
    while step < size:
        upper = (lane & step) != 0
        values = values + jnp.where(
            upper, pltpu.roll(values, step, 1), pltpu.roll(values, width - step, 1)
        )
        step *= 2
    return values


def exchange_kernel(
    owners, groups, candidates, tokens, keep,
    q_ref, pages_ref, owner_ref, slot_ref,
    loss_ref, qgrad_ref, back_ref, asked_ref,
    q_all, d_round, asked, asked_smem, send, fetched, turned, sums, rows_ref, weight_ref,
    shares, terms, q_part, q_got, kept,
    ask_out, ask_in, page_out, page_in, back_out, back_in,
    q_out, q_in, sum_out, sum_in, part_out, part_in, local_sem,
):
    kept = kept if keep else None
    me = lax.axis_index("pages")
    mine = lax.axis_index("query")
    page_count, patches, width = pages_ref.shape
    rows = q_ref.shape[0]

    def to_owner(k):
        return lax.rem(me + k, owners)

    def from_owner(k):
        return lax.rem(me + owners - k, owners)

    def to_group(k):
        return lax.rem(mine + k, groups)

    def from_group(k):
        return lax.rem(mine + groups - k, groups)

    def across_pages(src, dst, out, into, k):
        return pltpu.make_async_remote_copy(
            src_ref=src, dst_ref=dst, send_sem=out.at[k], recv_sem=into.at[k],
            device_id=(to_owner(k), mine), device_id_type=MESH,
        )

    def across_query(src, dst, out, into, k):
        return pltpu.make_async_remote_copy(
            src_ref=src, dst_ref=dst, send_sem=out.at[k], recv_sem=into.at[k],
            device_id=(me, to_group(k)), device_id_type=MESH,
        )

    def each(count, body):
        lax.fori_loop(1, count, lambda k, c: (body(k), c)[1], 0)

    barrier = pltpu.get_barrier_semaphore()
    each(owners, lambda k: pl.semaphore_signal(
        barrier, inc=1, device_id=(to_owner(k), mine), device_id_type=MESH))
    each(groups, lambda k: pl.semaphore_signal(
        barrier, inc=1, device_id=(me, to_group(k)), device_id_type=MESH))

    lane = lax.broadcasted_iota(jnp.int32, (1, LANES), 1)
    wanted = jnp.full((1, LANES), -1, jnp.int32)
    for c in range(candidates):
        wanted = jnp.where(lane == owner_ref[0, c], slot_ref[0, c], wanted)
    asked[me] = wanted
    q_unit, q_inv = normalize(q_ref[...])
    q_all[mine] = q_unit.astype(BF16)
    pl.semaphore_wait(barrier, owners + groups - 2)

    each(owners, lambda k: across_pages(asked.at[me], asked.at[me], ask_out, ask_in, k).start())
    each(groups, lambda k: across_query(q_all.at[mine], q_all.at[mine], q_out, q_in, k).start())

    def round_page(j, carry):
        d_round[j] = normalize(pages_ref[j])[0].astype(BF16)
        return carry

    lax.fori_loop(0, page_count, round_page, 0)

    def ask_arrived(k):
        across_pages(asked.at[from_owner(k)], asked.at[from_owner(k)], ask_out, ask_in, k).wait_recv()
        across_pages(asked.at[me], asked.at[me], ask_out, ask_in, k).wait_send()

    each(owners, ask_arrived)
    to_scalars = pltpu.make_async_copy(asked, asked_smem, local_sem)
    to_scalars.start()
    asked_ref[...] = asked[...]
    to_scalars.wait()

    def serve(k):
        to = to_owner(k)
        send[k, :patches] = d_round[jnp.maximum(asked_smem[to, 0, me], 0)]
        across_pages(
            send.at[k, pl.ds(0, patches)], fetched.at[me], page_out, page_in, k
        ).start()

    each(owners, serve)
    fetched[me] = d_round[jnp.maximum(asked_smem[me, 0, me], 0)]

    def query_arrived(k):
        across_query(q_all.at[from_group(k)], q_all.at[from_group(k)], q_out, q_in, k).wait_recv()
        across_query(q_all.at[mine], q_all.at[mine], q_out, q_in, k).wait_send()

    each(groups, query_arrived)

    def page_arrived(k):
        across_pages(
            send.at[k, pl.ds(0, patches)], fetched.at[from_owner(k)], page_out, page_in, k
        ).wait()

    each(owners, page_arrived)

    def exponentials(page, g):
        scores = lax.dot_general(
            page, q_all[g], (((1,), (1,)), ((), ())), preferred_element_type=F32
        )
        return jnp.exp2(scores * (SHARPNESS * math.log2(math.e)))

    def forward(c, carry):
        page = fetched[owner_ref[0, c]]
        turned[c] = page.T
        for g in range(groups):
            powers = exponentials(page, g)
            if kept is not None:
                kept[c, g] = powers
            sums[mine, c, :, g * rows : (g + 1) * rows] = jnp.sum(powers, axis=0, keepdims=True)
        return carry

    lax.fori_loop(0, candidates, forward, 0)
    each(groups, lambda k: across_query(sums.at[mine], sums.at[mine], sum_out, sum_in, k).start())

    def sums_arrived(k):
        across_query(sums.at[from_group(k)], sums.at[from_group(k)], sum_out, sum_in, k).wait_recv()
        across_query(sums.at[mine], sums.at[mine], sum_out, sum_in, k).wait_send()

    each(groups, sums_arrived)

    rows_ref[...] = jnp.ones_like(rows_ref)
    for c in range(candidates):
        total = sums[0, c]
        for g in range(1, groups):
            total = total + sums[g, c]
        rows_ref[c : c + 1, :] = total
    totals = rows_ref[...]
    logits = (INV_TEMP / SHARPNESS / tokens) * group_sums(jnp.log(totals), tokens)
    which = lax.broadcasted_iota(jnp.int32, totals.shape, 0)
    powers = jnp.where(which < candidates, jnp.exp(logits), 0.0)
    denominator = jnp.sum(powers, axis=0, keepdims=True)
    losses = jnp.log(denominator) - logits[0:1]
    positive = jnp.where(which == 0, 1.0, 0.0)
    weights = (LOSS_SCALE * INV_TEMP / tokens) * (powers / denominator - positive) / totals
    own = losses[:, :rows]
    for g in range(1, groups):
        own = jnp.where(mine == g, losses[:, g * rows : (g + 1) * rows], own)
    place = lax.broadcasted_iota(jnp.int32, (LANES, rows), 0)
    token = lax.broadcasted_iota(jnp.int32, (LANES, rows), 1)
    picked = jnp.sum(jnp.where(token == place * tokens, own, 0.0), axis=1, keepdims=True)
    loss_ref[...] = jnp.broadcast_to(picked, (LANES, LANES)).T[:1, : rows // tokens]
    for c in range(candidates):
        weight_ref[c] = weights[c : c + 1]

    def backward(c, carry):
        page = fetched[owner_ref[0, c]]
        term = jnp.zeros(page.shape, F32)
        for g in range(groups):
            powers = exponentials(page, g) if kept is None else kept[c, g]
            share = (weight_ref[c, :, g * rows : (g + 1) * rows] * powers).astype(BF16)
            shares[c, g] = share
            term = term + jnp.dot(share, q_all[g], preferred_element_type=F32)
        values = page.astype(F32)
        along = jnp.sum(values * term, axis=-1, keepdims=True).astype(BF16).astype(F32)
        terms[c, :patches] = (term - values * along).astype(BF16)
        flat = jnp.broadcast_to(along, term.shape).T
        pieces = [flat[:1, i : i + width] for i in range(0, patches, width)]
        pieces.append(jnp.zeros((TILE - len(pieces), width), F32))
        terms[c, patches:] = jnp.concatenate(pieces, axis=0).astype(BF16)
        return carry

    lax.fori_loop(0, candidates, backward, 0)

    def term_for(owner):
        place = jnp.int32(0)
        for c in range(candidates):
            place = jnp.where(owner_ref[0, c] == owner, c, place)
        return terms[place]

    def give_back(k):
        send[k] = term_for(to_owner(k))
        across_pages(send.at[k], back_ref.at[me], back_out, back_in, k).start()

    each(owners, give_back)
    back_ref[me] = term_for(me)

    for k in range(1, groups + 1):
        g = to_group(k)

        def query_side(c, total, g=g):
            return total + jnp.dot(turned[c], shares[c, g], preferred_element_type=F32)

        part = lax.fori_loop(0, candidates, query_side, jnp.zeros((width, rows), F32))
        across = q_all[g].T.astype(F32)
        if k < groups:
            along = jnp.sum(across * part, axis=0, keepdims=True).astype(BF16).astype(F32)
            q_part[k - 1, :width] = (part - across * along).astype(BF16)
            q_part[k - 1, width:] = jnp.broadcast_to(along, (TILE, rows)).astype(BF16)
            across_query(q_part.at[k - 1], q_got.at[k - 1], part_out, part_in, k).start()

    total = part
    for k in range(1, groups):
        across_query(q_part.at[k - 1], q_got.at[k - 1], part_out, part_in, k).wait()
        got = q_got[k - 1].astype(F32)
        total = total + (got[:width] + across * got[width : width + 1])
    q_unit, q_inv = normalize(q_ref[...])
    qgrad_ref[...] = unnormalize_grad(q_unit, q_inv, total.T)

    def back_arrived(k):
        across_pages(send.at[k], back_ref.at[from_owner(k)], back_out, back_in, k).wait()

    each(owners, back_arrived)


def finish_kernel(
    owners, asked_ref, pages_ref, back_ref, q_in_ref, loss_in_ref, loss_ref, q_out_ref, out_ref
):
    me = lax.axis_index("pages")
    page_count, patches, width = pages_ref.shape
    loss_ref[...] = loss_in_ref[...]
    q_out_ref[...] = q_in_ref[...]

    def clear(j, carry):
        out_ref[j] = jnp.zeros((patches, width), F32)
        return carry

    lax.fori_loop(0, page_count, clear, 0)

    def add(r, carry):
        slot = asked_ref[r, 0, me]

        @pl.when(slot >= 0)
        def _():
            d_unit, d_inv = normalize(pages_ref[slot])
            flat = back_ref[r, patches:].astype(F32)
            along = jnp.concatenate(
                [
                    jnp.broadcast_to(flat[i : i + 1], (width, width)).T
                    for i in range(patches // width)
                ],
                axis=0,
            )
            term = back_ref[r, :patches].astype(F32) + along * d_unit.astype(BF16).astype(F32)
            out_ref[slot] += unnormalize_grad(d_unit, d_inv, term)

        return carry

    lax.fori_loop(0, owners, add, 0)


def local(queries, pages, cand_owner, cand_slot):
    _, queries_local, tokens, width = queries.shape
    page_count, patches, _ = pages.shape
    owners = lax.axis_size("pages")
    groups = lax.axis_size("query")
    candidates = cand_owner.shape[1]
    rows = queries_local * tokens
    everyone = groups * rows
    padded = -(-candidates // 8) * 8
    assert queries_local <= LANES and owners <= LANES
    assert patches % width == 0 and patches // width < TILE and tokens & (tokens - 1) == 0
    grid = (candidates, groups, patches, rows)
    keep = 4 * math.prod(grid) <= KEEP_BYTES
    dma = pltpu.SemaphoreType.DMA
    vmem = pl.BlockSpec(memory_space=pltpu.VMEM)
    smem = pl.BlockSpec(memory_space=pltpu.SMEM)
    losses, query_grad, back, asked = pl.pallas_call(
        functools.partial(exchange_kernel, owners, groups, candidates, tokens, keep),
        out_shape=(
            jax.ShapeDtypeStruct((1, queries_local), F32),
            jax.ShapeDtypeStruct((rows, width), F32),
            jax.ShapeDtypeStruct((owners, patches + TILE, width), BF16),
            jax.ShapeDtypeStruct((owners, 1, LANES), jnp.int32),
        ),
        in_specs=[vmem, vmem, smem, smem],
        out_specs=(vmem, vmem, vmem, vmem),
        scratch_shapes=[
            pltpu.VMEM((groups, rows, width), BF16),
            pltpu.VMEM((page_count, patches, width), BF16),
            pltpu.VMEM((owners, 1, LANES), jnp.int32),
            pltpu.SMEM((owners, 1, LANES), jnp.int32),
            pltpu.VMEM((owners, patches + TILE, width), BF16),
            pltpu.VMEM((owners, patches, width), BF16),
            pltpu.VMEM((candidates, width, patches), BF16),
            pltpu.VMEM((groups, candidates, 1, everyone), F32),
            pltpu.VMEM((padded, everyone), F32),
            pltpu.VMEM((candidates, 1, everyone), F32),
            pltpu.VMEM(grid, BF16),
            pltpu.VMEM((candidates, patches + TILE, width), BF16),
            pltpu.VMEM((groups, width + TILE, rows), BF16),
            pltpu.VMEM((groups, width + TILE, rows), BF16),
            pltpu.VMEM(grid if keep else (8, LANES), F32),
        ]
        + [dma((owners,))] * 6
        + [dma((groups,))] * 6
        + [dma],
        compiler_params=pltpu.CompilerParams(
            collective_id=0, has_side_effects=True, vmem_limit_bytes=VMEM_BYTES
        ),
    )(queries.reshape(rows, width), pages, cand_owner, cand_slot)

    losses, query_grad, page_grad = pl.pallas_call(
        functools.partial(finish_kernel, owners),
        out_shape=(
            jax.ShapeDtypeStruct(losses.shape, F32),
            jax.ShapeDtypeStruct(query_grad.shape, F32),
            jax.ShapeDtypeStruct((page_count, patches, width), F32),
        ),
        in_specs=[smem, vmem, vmem, vmem, vmem],
        out_specs=(vmem, vmem, vmem),
        compiler_params=pltpu.CompilerParams(vmem_limit_bytes=VMEM_BYTES),
    )(asked, pages, back, query_grad, losses)
    return (
        losses,
        query_grad.reshape(1, queries_local, tokens, width),
        page_grad,
    )


def solution(mesh):
    return jax.shard_map(
        local,
        mesh=mesh,
        in_specs=(
            P("pages", "query", None, None),
            P("pages", "query", None),
            P("pages", None),
            P("pages", None),
        ),
        out_specs=(P("pages", "query"), P("pages", "query", None, None), P("pages", "query", None)),
        check_vma=False,
    )
```

```python
import functools
import math

import jax
import jax.numpy as jnp
from jax import lax
from jax.experimental import pallas as pl
from jax.experimental.pallas import tpu as pltpu
from jax.sharding import PartitionSpec as P

SHARPNESS = 10.0
INV_TEMP = 20.0
LOSS_SCALE = 256.0
EPSILON = 1e-06
LANES = 128
MESH = pl.DeviceIdType.MESH
VMEM_BYTES = 56 * 2**20
KEEP_BYTES = 8 * 2**20
TILE = 16
F32 = jnp.float32
BF16 = jnp.bfloat16


def normalize(embeddings):
    values = embeddings.astype(F32)
    inverse = lax.rsqrt(jnp.sum(values * values, axis=-1, keepdims=True) + EPSILON)
    return values * inverse, inverse


def unnormalize_grad(unit_vectors, inverse, gradient):
    return inverse * (
        gradient - unit_vectors * jnp.sum(unit_vectors * gradient, axis=-1, keepdims=True)
    )


def group_sums(values, size):
    width = values.shape[1]
    lane = lax.broadcasted_iota(jnp.int32, values.shape, 1)
    step = 1
    while step < size:
        upper = (lane & step) != 0
        values = values + jnp.where(
            upper, pltpu.roll(values, step, 1), pltpu.roll(values, width - step, 1)
        )
        step *= 2
    return values


def exchange_kernel(
    owners, groups, candidates, tokens, keep,
    q_ref, pages_ref, owner_ref, slot_ref,
    loss_ref, qgrad_ref, back_ref, asked_ref,
    q_all, d_round, asked, asked_smem, send, fetched, turned, sums, rows_ref, weight_ref,
    shares, terms, q_part, q_got, kept,
    ask_out, ask_in, page_out, page_in, back_out, back_in,
    q_out, q_in, sum_out, sum_in, part_out, part_in, local_sem,
):
    kept = kept if keep else None
    me = lax.axis_index("pages")
    mine = lax.axis_index("query")
    page_count, patches, width = pages_ref.shape
    rows = q_ref.shape[0]

    def to_owner(k):
        return lax.rem(me + k, owners)

    def from_owner(k):
        return lax.rem(me + owners - k, owners)

    def to_group(k):
        return lax.rem(mine + k, groups)

    def from_group(k):
        return lax.rem(mine + groups - k, groups)

    def across_pages(src, dst, out, into, k):
        return pltpu.make_async_remote_copy(
            src_ref=src, dst_ref=dst, send_sem=out.at[k], recv_sem=into.at[k],
            device_id=(to_owner(k), mine), device_id_type=MESH,
        )

    def across_query(src, dst, out, into, k):
        return pltpu.make_async_remote_copy(
            src_ref=src, dst_ref=dst, send_sem=out.at[k], recv_sem=into.at[k],
            device_id=(me, to_group(k)), device_id_type=MESH,
        )

    def each(count, body):
        lax.fori_loop(1, count, lambda k, c: (body(k), c)[1], 0)

    barrier = pltpu.get_barrier_semaphore()
    each(owners, lambda k: pl.semaphore_signal(
        barrier, inc=1, device_id=(to_owner(k), mine), device_id_type=MESH))
    each(groups, lambda k: pl.semaphore_signal(
        barrier, inc=1, device_id=(me, to_group(k)), device_id_type=MESH))

    lane = lax.broadcasted_iota(jnp.int32, (1, LANES), 1)
    wanted = jnp.full((1, LANES), -1, jnp.int32)
    for c in range(candidates):
        wanted = jnp.where(lane == owner_ref[0, c], slot_ref[0, c], wanted)
    asked[me] = wanted
    q_unit, q_inv = normalize(q_ref[...])
    q_all[mine] = q_unit.astype(BF16)
    pl.semaphore_wait(barrier, owners + groups - 2)

    each(owners, lambda k: across_pages(asked.at[me], asked.at[me], ask_out, ask_in, k).start())
    each(groups, lambda k: across_query(q_all.at[mine], q_all.at[mine], q_out, q_in, k).start())

    def round_page(j, carry):
        d_round[j] = normalize(pages_ref[j])[0].astype(BF16)
        return carry

    lax.fori_loop(0, page_count, round_page, 0)

    def ask_arrived(k):
        across_pages(asked.at[from_owner(k)], asked.at[from_owner(k)], ask_out, ask_in, k).wait_recv()
        across_pages(asked.at[me], asked.at[me], ask_out, ask_in, k).wait_send()

    each(owners, ask_arrived)
    to_scalars = pltpu.make_async_copy(asked, asked_smem, local_sem)
    to_scalars.start()
    asked_ref[...] = asked[...]
    to_scalars.wait()

    def serve(k):
        to = to_owner(k)
        send[k, :patches] = d_round[jnp.maximum(asked_smem[to, 0, me], 0)]
        across_pages(
            send.at[k, pl.ds(0, patches)], fetched.at[me], page_out, page_in, k
        ).start()

    each(owners, serve)
    fetched[me] = d_round[jnp.maximum(asked_smem[me, 0, me], 0)]

    def query_arrived(k):
        across_query(q_all.at[from_group(k)], q_all.at[from_group(k)], q_out, q_in, k).wait_recv()
        across_query(q_all.at[mine], q_all.at[mine], q_out, q_in, k).wait_send()

    each(groups, query_arrived)

    def page_arrived(k):
        across_pages(
            send.at[k, pl.ds(0, patches)], fetched.at[from_owner(k)], page_out, page_in, k
        ).wait()

    each(owners, page_arrived)

    def exponentials(page, g):
        scores = lax.dot_general(
            page, q_all[g], (((1,), (1,)), ((), ())), preferred_element_type=F32
        )
        return jnp.exp2(scores * (SHARPNESS * math.log2(math.e)))

    def forward(c, carry):
        page = fetched[owner_ref[0, c]]
        turned[c] = page.T
        for g in range(groups):
            powers = exponentials(page, g)
            if kept is not None:
                kept[c, g] = powers
            sums[mine, c, :, g * rows : (g + 1) * rows] = jnp.sum(powers, axis=0, keepdims=True)
        return carry

    lax.fori_loop(0, candidates, forward, 0, unroll=candidates <= 4)
    each(groups, lambda k: across_query(sums.at[mine], sums.at[mine], sum_out, sum_in, k).start())

    def sums_arrived(k):
        across_query(sums.at[from_group(k)], sums.at[from_group(k)], sum_out, sum_in, k).wait_recv()
        across_query(sums.at[mine], sums.at[mine], sum_out, sum_in, k).wait_send()

    each(groups, sums_arrived)

    rows_ref[...] = jnp.ones_like(rows_ref)
    for c in range(candidates):
        total = sums[0, c]
        for g in range(1, groups):
            total = total + sums[g, c]
        rows_ref[c : c + 1, :] = total
    totals = rows_ref[...]
    logits = (INV_TEMP / SHARPNESS / tokens) * group_sums(jnp.log(totals), tokens)
    which = lax.broadcasted_iota(jnp.int32, totals.shape, 0)
    powers = jnp.where(which < candidates, jnp.exp(logits), 0.0)
    denominator = jnp.sum(powers, axis=0, keepdims=True)
    losses = jnp.log(denominator) - logits[0:1]
    positive = jnp.where(which == 0, 1.0, 0.0)
    weights = (LOSS_SCALE * INV_TEMP / tokens) * (powers / denominator - positive) / totals
    own = losses[:, :rows]
    for g in range(1, groups):
        own = jnp.where(mine == g, losses[:, g * rows : (g + 1) * rows], own)
    place = lax.broadcasted_iota(jnp.int32, (LANES, rows), 0)
    token = lax.broadcasted_iota(jnp.int32, (LANES, rows), 1)
    picked = jnp.sum(jnp.where(token == place * tokens, own, 0.0), axis=1, keepdims=True)
    loss_ref[...] = jnp.broadcast_to(picked, (LANES, LANES)).T[:1, : rows // tokens]
    for c in range(candidates):
        weight_ref[c] = weights[c : c + 1]

    def backward(c, carry):
        page = fetched[owner_ref[0, c]]
        term = jnp.zeros(page.shape, F32)
        for g in range(groups):
            powers = exponentials(page, g) if kept is None else kept[c, g]
            share = (weight_ref[c, :, g * rows : (g + 1) * rows] * powers).astype(BF16)
            shares[c, g] = share
            term = term + jnp.dot(share, q_all[g], preferred_element_type=F32)
        values = page.astype(F32)
        along = jnp.sum(values * term, axis=-1, keepdims=True).astype(BF16).astype(F32)
        terms[c, :patches] = (term - values * along).astype(BF16)
        flat = jnp.broadcast_to(along, term.shape).T
        pieces = [flat[:1, i : i + width] for i in range(0, patches, width)]
        pieces.append(jnp.zeros((TILE - len(pieces), width), F32))
        terms[c, patches:] = jnp.concatenate(pieces, axis=0).astype(BF16)
        return carry

    lax.fori_loop(0, candidates, backward, 0, unroll=candidates <= 4)

    def term_for(owner):
        place = jnp.int32(0)
        for c in range(candidates):
            place = jnp.where(owner_ref[0, c] == owner, c, place)
        return terms[place]

    def give_back(k):
        send[k] = term_for(to_owner(k))
        across_pages(send.at[k], back_ref.at[me], back_out, back_in, k).start()

    each(owners, give_back)
    back_ref[me] = term_for(me)

    for k in range(1, groups + 1):
        g = to_group(k)

        def query_side(c, total, g=g):
            return total + jnp.dot(turned[c], shares[c, g], preferred_element_type=F32)

        part = lax.fori_loop(0, candidates, query_side, jnp.zeros((width, rows), F32), unroll=candidates <= 4)
        across = q_all[g].T.astype(F32)
        if k < groups:
            along = jnp.sum(across * part, axis=0, keepdims=True).astype(BF16).astype(F32)
            q_part[k - 1, :width] = (part - across * along).astype(BF16)
            q_part[k - 1, width:] = jnp.broadcast_to(along, (TILE, rows)).astype(BF16)
            across_query(q_part.at[k - 1], q_got.at[k - 1], part_out, part_in, k).start()

    total = part
    for k in range(1, groups):
        across_query(q_part.at[k - 1], q_got.at[k - 1], part_out, part_in, k).wait()
        got = q_got[k - 1].astype(F32)
        total = total + (got[:width] + across * got[width : width + 1])
    q_unit, q_inv = normalize(q_ref[...])
    qgrad_ref[...] = unnormalize_grad(q_unit, q_inv, total.T)

    def back_arrived(k):
        across_pages(send.at[k], back_ref.at[from_owner(k)], back_out, back_in, k).wait()

    each(owners, back_arrived)


def finish_kernel(
    owners, asked_ref, pages_ref, back_ref, q_in_ref, loss_in_ref, loss_ref, q_out_ref, out_ref
):
    me = lax.axis_index("pages")
    page_count, patches, width = pages_ref.shape
    loss_ref[...] = loss_in_ref[...]
    q_out_ref[...] = q_in_ref[...]

    def clear(j, carry):
        out_ref[j] = jnp.zeros((patches, width), F32)
        return carry

    lax.fori_loop(0, page_count, clear, 0)

    def add(r, carry):
        slot = asked_ref[r, 0, me]

        @pl.when(slot >= 0)
        def _():
            d_unit, d_inv = normalize(pages_ref[slot])
            flat = back_ref[r, patches:].astype(F32)
            along = jnp.concatenate(
                [
                    jnp.broadcast_to(flat[i : i + 1], (width, width)).T
                    for i in range(patches // width)
                ],
                axis=0,
            )
            term = back_ref[r, :patches].astype(F32) + along * d_unit.astype(BF16).astype(F32)
            out_ref[slot] += unnormalize_grad(d_unit, d_inv, term)

        return carry

    lax.fori_loop(0, owners, add, 0)


def local(queries, pages, cand_owner, cand_slot):
    _, queries_local, tokens, width = queries.shape
    page_count, patches, _ = pages.shape
    owners = lax.axis_size("pages")
    groups = lax.axis_size("query")
    candidates = cand_owner.shape[1]
    rows = queries_local * tokens
    everyone = groups * rows
    padded = -(-candidates // 8) * 8
    assert queries_local <= LANES and owners <= LANES
    assert patches % width == 0 and patches // width < TILE and tokens & (tokens - 1) == 0
    grid = (candidates, groups, patches, rows)
    keep = 4 * math.prod(grid) <= KEEP_BYTES
    dma = pltpu.SemaphoreType.DMA
    vmem = pl.BlockSpec(memory_space=pltpu.VMEM)
    smem = pl.BlockSpec(memory_space=pltpu.SMEM)
    losses, query_grad, back, asked = pl.pallas_call(
        functools.partial(exchange_kernel, owners, groups, candidates, tokens, keep),
        out_shape=(
            jax.ShapeDtypeStruct((1, queries_local), F32),
            jax.ShapeDtypeStruct((rows, width), F32),
            jax.ShapeDtypeStruct((owners, patches + TILE, width), BF16),
            jax.ShapeDtypeStruct((owners, 1, LANES), jnp.int32),
        ),
        in_specs=[vmem, vmem, smem, smem],
        out_specs=(vmem, vmem, vmem, vmem),
        scratch_shapes=[
            pltpu.VMEM((groups, rows, width), BF16),
            pltpu.VMEM((page_count, patches, width), BF16),
            pltpu.VMEM((owners, 1, LANES), jnp.int32),
            pltpu.SMEM((owners, 1, LANES), jnp.int32),
            pltpu.VMEM((owners, patches + TILE, width), BF16),
            pltpu.VMEM((owners, patches, width), BF16),
            pltpu.VMEM((candidates, width, patches), BF16),
            pltpu.VMEM((groups, candidates, 1, everyone), F32),
            pltpu.VMEM((padded, everyone), F32),
            pltpu.VMEM((candidates, 1, everyone), F32),
            pltpu.VMEM(grid, BF16),
            pltpu.VMEM((candidates, patches + TILE, width), BF16),
            pltpu.VMEM((groups, width + TILE, rows), BF16),
            pltpu.VMEM((groups, width + TILE, rows), BF16),
            pltpu.VMEM(grid if keep else (8, LANES), F32),
        ]
        + [dma((owners,))] * 6
        + [dma((groups,))] * 6
        + [dma],
        compiler_params=pltpu.CompilerParams(
            collective_id=0, has_side_effects=True, vmem_limit_bytes=VMEM_BYTES
        ),
    )(queries.reshape(rows, width), pages, cand_owner, cand_slot)

    losses, query_grad, page_grad = pl.pallas_call(
        functools.partial(finish_kernel, owners),
        out_shape=(
            jax.ShapeDtypeStruct(losses.shape, F32),
            jax.ShapeDtypeStruct(query_grad.shape, F32),
            jax.ShapeDtypeStruct((page_count, patches, width), F32),
        ),
        in_specs=[smem, vmem, vmem, vmem, vmem],
        out_specs=(vmem, vmem, vmem),
        compiler_params=pltpu.CompilerParams(vmem_limit_bytes=VMEM_BYTES),
    )(asked, pages, back, query_grad, losses)
    return (
        losses,
        query_grad.reshape(1, queries_local, tokens, width),
        page_grad,
    )


def solution(mesh):
    return jax.shard_map(
        local,
        mesh=mesh,
        in_specs=(
            P("pages", "query", None, None),
            P("pages", "query", None),
            P("pages", None),
            P("pages", None),
        ),
        out_specs=(P("pages", "query"), P("pages", "query", None, None), P("pages", "query", None)),
        check_vma=False,
    )
```
